32 devices in a mesh: grp: 2 (over y), row: 4 (over z), ch: 2 (over x), sub: 2 (over core).
Axes of the slice: x: 2, y: 2, z: 4, core: 2. Of those that a mesh axis runs over, the one named last changes fastest.
Arguments:
- pair_act: bfloat16 [128, 256, 128], P('ch', ('grp', 'row'), 'sub'), parts along dimension 1, may hold values from -6 to 6
- token_mask: int32 [256], P('grp'), parts along dimension 0, may hold values 0 or 1
- norm_gain: float32 [128], replicated, may hold values from 0.1 to 1.9
- norm_shift: float32 [128], replicated, may hold values from -2.5 to 2.5
- proj_weight: bfloat16 [128, 256], replicated, may hold values from -0.5 to 0.5
- gate_weight: bfloat16 [128, 256], replicated, may hold values from -0.5 to 0.5
- outgate_weight: bfloat16 [128, 128], replicated, may hold values from -0.5 to 0.5
- post_gain: float32 [128], replicated, may hold values from 0.1 to 1.9
- post_shift: float32 [128], replicated, may hold values from -2.5 to 2.5
- out_weight: bfloat16 [128, 128], replicated, may hold values from -0.5 to 0.5
Outputs:
- update: bfloat16 [128, 256, 128], P('ch', ('grp', 'row'), 'sub'), parts along dimension 1
The draws below stay inside these ranges and needn't reach their ends.
There are 2 independent parts, one for each index of `grp`. The reference program is written for one: setup_inputs(seed, part) draws one part's arguments, and reference() takes and returns one part's arrays. A program takes and returns all parts, laid end to end along the dimension named above; an argument that names none is the same for every part. Nothing has to cross between parts.
All inputs are finite; a program needn't handle non-finite values.
Results may differ from the reference program's by a relative error of at most 0.0062.
Values may be sent and summed in bfloat16 or wider, within the bound.
A program may use at most 64 MiB of HBM per device.

```python
import jax
import jax.numpy as jnp
from jax import lax

C = 128
H = 128
N = 128


def set_ends(drawn, rng, least, top_value):
    longest = drawn.shape.index(max(drawn.shape))
    spots = []
    for shift in (0, 1):
        where = [jax.random.randint(jax.random.fold_in(rng, axis), (), 0, length) for axis, length in enumerate(drawn.shape)]
        where[longest] = (where[longest] + shift) % drawn.shape[longest]
        spots.append(tuple(where))
    return drawn.at[spots[0]].set(least).at[spots[1]].set(top_value)


def shard_levels(stream_key, shape, pieces, smallest, largest):
    level, own = 1.0, jax.random.fold_in(stream_key, 6)
    for dim, parts in pieces:
        heights = jnp.exp(jax.random.uniform(jax.random.fold_in(own, dim), (parts,), jnp.float32, smallest / len(pieces), largest / len(pieces)))
        level = level * jnp.repeat(heights, shape[dim] // parts).reshape([-1 if axis == dim else 1 for axis in range(len(shape))])
    return level


def bell_draw(stream_key, shape, spread, most, shards=(), kind=jnp.bfloat16):
    entries = jax.random.normal(stream_key, shape, jnp.float32) * spread
    if len(shards) > 0:
        entries = shard_levels(stream_key, shape, shards, -0.22, 0.18) * entries
    return jnp.clip(entries, min=-most, max=most).astype(kind)


def setup_inputs(seed: int = 0, part: int = 0) -> dict:
    keys = jax.random.split(jax.random.key(seed), 11)
    part_keys = jax.random.split(jax.random.fold_in(keys[10], part), 11)
    pair_act = bell_draw(part_keys[0], (C, N, N), 1.0, 6.0, ((0, 2), (1, 4), (2, 2)))
    token_mask = set_ends((jax.random.randint(part_keys[1], (N,), 0, 8) < 7).astype(jnp.int32), jax.random.fold_in(part_keys[1], 1), 0, 1)
    norm_gain = jnp.clip(1.0 + 0.18 * jax.random.normal(keys[2], (C,), jnp.float32), 0.1, 1.9)
    norm_shift = bell_draw(keys[3], (C,), 0.5, 2.5, (), jnp.float32)
    proj_weight = bell_draw(keys[4], (C, 2 * H), C ** -0.5, 0.5)
    gate_weight = bell_draw(keys[5], (C, 2 * H), C ** -0.5, 0.5)
    outgate_weight = bell_draw(keys[6], (C, C), C ** -0.5, 0.5)
    post_gain = jnp.clip(1.0 + 0.18 * jax.random.normal(keys[7], (H,), jnp.float32), 0.1, 1.9)
    post_shift = bell_draw(keys[8], (H,), 0.5, 2.5, (), jnp.float32)
    out_weight = bell_draw(keys[9], (H, C), H ** -0.5, 0.5)
    return dict(pair_act=pair_act, token_mask=token_mask, norm_gain=norm_gain, norm_shift=norm_shift, proj_weight=proj_weight, gate_weight=gate_weight, outgate_weight=outgate_weight, post_gain=post_gain, post_shift=post_shift, out_weight=out_weight)


def layer_norm(values, gain, shift):
    widened = values.astype(jnp.float32)
    average = lax.optimization_barrier(jnp.mean(widened, axis=0, keepdims=True))
    centered = widened - average
    variance = lax.optimization_barrier(jnp.mean(centered * centered, axis=0, keepdims=True))
    scaled = centered * jax.lax.rsqrt(variance + 1e-05)
    return (scaled * gain[:, None, None] + shift[:, None, None]).astype(jnp.bfloat16)

def reference(pair_act, token_mask, norm_gain, norm_shift, proj_weight, gate_weight, outgate_weight, post_gain, post_shift, out_weight):
    normed = layer_norm(pair_act, norm_gain, norm_shift)
    wide_normed = normed.astype(jnp.float32)
    masked = token_mask.astype(jnp.float32)
    pair_mask = masked[:, None] * masked[None, :]
    projected = jnp.einsum('ce,cij->eij', proj_weight.astype(jnp.float32), wide_normed)
    gated = jnp.einsum('ce,cij->eij', gate_weight.astype(jnp.float32), wide_normed)
    left = (projected[:H] * jax.nn.sigmoid(gated[:H]) * pair_mask).astype(jnp.bfloat16)
    right = (projected[H:] * jax.nn.sigmoid(gated[H:]) * pair_mask).astype(jnp.bfloat16)
    triangle = jnp.einsum('hik,hjk->hij', left.astype(jnp.float32), right.astype(jnp.float32)).astype(jnp.bfloat16)
    post = layer_norm(triangle, post_gain, post_shift)
    outgate = jax.nn.sigmoid(jnp.einsum('dc,dij->cij', outgate_weight.astype(jnp.float32), wide_normed))
    projected_out = jnp.einsum('hc,hij->cij', out_weight.astype(jnp.float32), post.astype(jnp.float32))
    return (projected_out * outgate).astype(jnp.bfloat16)
```

```python
import functools

import jax
import jax.numpy as jnp
from jax import lax
from jax.experimental import pallas as pl
from jax.experimental.pallas import tpu as pltpu
from jax.sharding import PartitionSpec as P


def layer_norm(values, gain, shift):
    widened = values.astype(jnp.float32)
    average = jnp.mean(widened, axis=0, keepdims=True)
    centered = widened - average
    variance = jnp.mean(centered * centered, axis=0, keepdims=True)
    scaled = centered * lax.rsqrt(variance + 1e-05)
    spread = (gain.shape[0],) + (1,) * (values.ndim - 1)
    return (scaled * gain.reshape(spread) + shift.reshape(spread)).astype(jnp.bfloat16)


def gated_inputs(normed, weights, pair_mask, hidden):
    projected = jnp.einsum("ce,c...->e...", weights, normed, preferred_element_type=jnp.float32)
    left_panel = (
        projected[:hidden] * jax.nn.sigmoid(projected[2 * hidden : 3 * hidden]) * pair_mask
    ).astype(jnp.bfloat16)
    right_panel = (
        projected[hidden : 2 * hidden]
        * jax.nn.sigmoid(projected[3 * hidden : 4 * hidden])
        * pair_mask
    ).astype(jnp.bfloat16)
    outgate = jax.nn.sigmoid(projected[4 * hidden :])
    return (left_panel, right_panel, outgate)


def contract(left_panel, right_panel):
    partial_sums = jnp.einsum(
        "hik,hjk->hij",
        left_panel,
        lax.all_gather(right_panel, "row", axis=1, tiled=True),
        preferred_element_type=jnp.float32,
    )
    return lax.psum_scatter(partial_sums, "sub", scatter_dimension=2, tiled=True).astype(
        jnp.bfloat16
    )


def body(
    pair_act,
    token_mask,
    norm_gain,
    norm_shift,
    proj_weight,
    gate_weight,
    outgate_weight,
    post_gain,
    post_shift,
    out_weight,
):
    slab_rows = pair_act.shape[1]
    slab_cols = pair_act.shape[2]
    hidden = out_weight.shape[0]
    channels = out_weight.shape[1]
    chan_count = lax.axis_size("ch")
    chan_index = lax.axis_index("ch")
    masked = token_mask.astype(jnp.float32)
    row_mask = lax.dynamic_slice_in_dim(masked, lax.axis_index("row") * slab_rows, slab_rows, 0)
    col_start = lax.axis_index("sub") * slab_cols
    gathered = lax.all_gather(pair_act, "ch", axis=0, tiled=True)
    normed = layer_norm(gathered, norm_gain, norm_shift)
    col_mask = lax.dynamic_slice_in_dim(masked, col_start, slab_cols, 0)
    pair_mask = row_mask[:, None] * col_mask[None, :]
    hid_part = hidden // chan_count
    out_part = channels // chan_count
    hid_start = chan_index * hid_part
    out_start = chan_index * out_part
    weights = jnp.concatenate(
        [
            lax.dynamic_slice_in_dim(proj_weight, hid_start, hid_part, 1),
            lax.dynamic_slice_in_dim(proj_weight, hidden + hid_start, hid_part, 1),
            lax.dynamic_slice_in_dim(gate_weight, hid_start, hid_part, 1),
            lax.dynamic_slice_in_dim(gate_weight, hidden + hid_start, hid_part, 1),
            lax.dynamic_slice_in_dim(outgate_weight, out_start, out_part, 1),
        ],
        axis=1,
    )
    left_panel, right_panel, outgate = gated_inputs(normed, weights, pair_mask, hid_part)
    triangle = contract(left_panel, right_panel)
    all_hidden = lax.all_gather(triangle, "ch", axis=0, tiled=True)
    post = layer_norm(all_hidden, post_gain, post_shift)
    out_slice = lax.dynamic_slice_in_dim(out_weight, out_start, out_part, 1)
    projected_out = jnp.einsum("hc,hij->cij", out_slice, post, preferred_element_type=jnp.float32)
    return (projected_out * outgate).astype(jnp.bfloat16)


MESH = pl.DeviceIdType.MESH
LANES = 128
HALF = 64
CHUNKS = 4


def column(row):
    return jnp.transpose(jnp.broadcast_to(row.astype(jnp.float32), (LANES, LANES)))


def spread_gain(panel, lanes):
    return jnp.concatenate([panel] * (lanes // LANES), axis=1)


def swish_gate(values):
    return 0.5 * jnp.tanh(0.5 * values) + 0.5


def normalise(values, gain, shift):
    average = jnp.mean(values, axis=0, keepdims=True)
    centered = values - average
    variance = jnp.mean(centered * centered, axis=0, keepdims=True)
    scaled = centered * lax.rsqrt(variance + 1e-05)
    return (scaled * gain + shift).astype(jnp.bfloat16)


def fused_kernel(
    rows,
    x_ref,
    mask_ref,
    norm_gain,
    norm_shift,
    proj_ref,
    gate_ref,
    outgate_ref,
    post_gain,
    post_shift,
    out_weight,
    o_ref,
    x_all,
    weights,
    turned,
    columns,
    gate_keep,
    send_buf,
    recv_buf,
    wide,
    panels,
    tri_wide,
    tri_send,
    tri_all,
    local_sem,
    x_send,
    x_recv,
    a_send,
    a_recv,
    t_send,
    t_recv,
    f_send,
    f_recv,
):
    row = lax.axis_index("row")
    ch = lax.axis_index("ch")
    sub = lax.axis_index("sub")
    dests = 2 * rows
    me = row * 2 + sub
    other_ch = 1 - ch
    tiles = x_ref.shape[1] // LANES
    per = tiles // CHUNKS
    width = per * LANES

    def peer(offset):
        d = lax.rem(me + offset, dests)
        return d, {"row": d // 2, "sub": lax.rem(d, 2)}

    barrier = pltpu.get_barrier_semaphore()
    pl.semaphore_signal(barrier, inc=1, device_id={"ch": other_ch}, device_id_type=MESH)
    for offset in range(1, dests):
        pl.semaphore_signal(barrier, inc=1, device_id=peer(offset)[1], device_id_type=MESH)

    own_rows = pl.ds(pl.multiple_of(ch * HALF, HALF), HALF)
    local = pltpu.make_async_copy(x_ref, x_all.at[own_rows], local_sem)
    local.start()
    pl.semaphore_wait(barrier, dests)
    x_copies = []
    for k in range(CHUNKS):
        cells = pl.ds(k * width, width)
        copy = pltpu.make_async_remote_copy(
            src_ref=x_ref.at[:, cells],
            dst_ref=x_all.at[own_rows, cells],
            send_sem=x_send.at[k],
            recv_sem=x_recv.at[k],
            device_id={"ch": other_ch},
            device_id_type=MESH,
        )
        copy.start()
        x_copies.append(copy)

    for at, ref in ((0, proj_ref), (256, gate_ref), (512, outgate_ref), (640, out_weight)):
        turned[at : at + ref.shape[1], :] = jnp.transpose(ref[...].astype(jnp.float32))
    for slot, base in enumerate((0, 128, 256, 384, 512, 640)):
        rows_here = pl.ds(pl.multiple_of(base + ch * HALF, HALF), HALF)
        weights[slot * HALF : (slot + 1) * HALF, :] = turned[rows_here, :].astype(jnp.bfloat16)
    gain = column(norm_gain[...])
    shift = column(norm_shift[...])
    lane = lax.broadcasted_iota(jnp.int32, (16, LANES), 1)
    low = lane < HALF
    mask_row = mask_ref[...].astype(jnp.float32)
    columns[...] = column(mask_row)
    mask_wide = jnp.broadcast_to(mask_row, (16, LANES))
    mask_turn = pltpu.roll(mask_wide, HALF, 1)
    near = jnp.where(low, mask_wide, mask_turn)
    far = jnp.where(low, mask_turn, mask_wide)
    second = sub.astype(jnp.float32)
    col_mask = near * (1.0 - second) + far * second
    row_at = pl.multiple_of(row * 32, 32)
    row_mask = jnp.where(low, columns[pl.ds(row_at, 16), :], columns[pl.ds(row_at + 16, 16), :])
    pair_mask = row_mask * col_mask

    local.wait()
    gain_wide = spread_gain(gain, width)
    shift_wide = spread_gain(shift, width)
    a_copies = []
    for k in range(CHUNKS):
        cells = pl.ds(k * width, width)
        x_copies[k].wait_recv()
        normed = normalise(x_all[:, cells].astype(jnp.float32), gain_wide, shift_wide)
        projected = jnp.dot(weights[: 5 * HALF, :], normed, preferred_element_type=jnp.float32)
        gate_keep[:, cells] = swish_gate(projected[4 * HALF :])
        both = projected[: 2 * HALF] * swish_gate(projected[2 * HALF : 4 * HALF])
        for t in range(per):
            tile = k * per + t
            block = both[:, t * LANES : (t + 1) * LANES] * pair_mask[tile : tile + 1, :]
            for d in range(dests):
                pair = jnp.concatenate(
                    [block[8 * d : 8 * d + 8], block[HALF + 8 * d : HALF + 8 * d + 8]], axis=0
                )
                send_buf[d, tile * 16 : tile * 16 + 16, :] = pair.astype(jnp.bfloat16)
        span = pl.ds(k * per * 16, per * 16)
        for offset in range(1, dests):
            d, where = peer(offset)
            copy = pltpu.make_async_remote_copy(
                src_ref=send_buf.at[d, span],
                dst_ref=recv_buf.at[me, span],
                send_sem=a_send.at[offset, k],
                recv_sem=a_recv.at[offset, k],
                device_id=where,
                device_id_type=MESH,
            )
            copy.start()
            a_copies.append(copy)
    recv_buf[me] = send_buf[me]
    post_gain_wide = spread_gain(column(post_gain[...]), width)
    post_shift_wide = spread_gain(column(post_shift[...]), width)
    for copy in a_copies:
        copy.wait_recv()

    for r in range(rows):
        for s in range(2):
            wide[s] = recv_buf[2 * r + s].astype(jnp.float32)
        for e in range(16):
            first = wide[0, pl.ds(e, 16, stride=16), :]
            last = wide[1, pl.ds(e, 16, stride=16), :]
            top = jnp.where(low, first, pltpu.roll(last, HALF, 1))
            bottom = jnp.where(low, pltpu.roll(first, HALF, 1), last)
            panels[e, 32 * r : 32 * r + 16, :] = top.astype(jnp.bfloat16)
            panels[e, 32 * r + 16 : 32 * r + 32, :] = bottom.astype(jnp.bfloat16)

    for h in range(8):
        tri = lax.dot_general(
            panels[h], panels[8 + h], (((1,), (1,)), ((), ())), preferred_element_type=jnp.float32
        )
        rolled = pltpu.roll(tri, HALF, 1)
        for r in range(rows):
            a, b = slice(32 * r, 32 * r + 16), slice(32 * r + 16, 32 * r + 32)
            tri_wide[2 * r, pl.ds(h, 16, stride=8), :] = jnp.where(low, tri[a], rolled[b])
            tri_wide[2 * r + 1, pl.ds(h, 16, stride=8), :] = jnp.where(low, rolled[a], tri[b])

    tri_send[...] = tri_wide[...].astype(jnp.bfloat16)
    t_copies = []
    for offset in range(1, dests):
        d, where = peer(offset)
        copy = pltpu.make_async_remote_copy(
            src_ref=tri_send.at[d],
            dst_ref=tri_all.at[ch, me],
            send_sem=t_send.at[offset],
            recv_sem=t_recv.at[offset],
            device_id=where,
            device_id_type=MESH,
        )
        copy.start()
        t_copies.append(copy)
    tri_all[ch, me] = tri_send[me]
    f_copies = []
    for offset in range(dests):
        if offset > 0:
            t_copies[offset - 1].wait_recv()
        source = lax.rem(me + dests - offset, dests)
        copy = pltpu.make_async_remote_copy(
            src_ref=tri_all.at[ch, source],
            dst_ref=tri_all.at[ch, source],
            send_sem=f_send.at[offset],
            recv_sem=f_recv.at[offset],
            device_id={"ch": other_ch},
            device_id_type=MESH,
        )
        copy.start()
        f_copies.append(copy)
    for copy in f_copies:
        copy.wait_recv()

    for k in range(CHUNKS):
        cells = pl.ds(k * width, width)
        parts = []
        for t in range(k * per, (k + 1) * per):
            stack = [
                tri_all[c, q, t * 8 : t * 8 + 8, :].astype(jnp.float32)
                for c in range(2)
                for q in range(dests)
            ]
            parts.append(jnp.concatenate(stack, axis=0))
        post = normalise(jnp.concatenate(parts, axis=1), post_gain_wide, post_shift_wide)
        update = jnp.dot(weights[5 * HALF :, :], post, preferred_element_type=jnp.float32)
        o_ref[:, cells] = (update * gate_keep[:, cells]).astype(jnp.bfloat16)
    for copy in x_copies + a_copies + t_copies + f_copies:
        copy.wait_send()


def fused_body(
    pair_act,
    token_mask,
    norm_gain,
    norm_shift,
    proj_weight,
    gate_weight,
    outgate_weight,
    post_gain,
    post_shift,
    out_weight,
):
    rows = lax.axis_size("row")
    dests = 2 * rows
    chan, slab_rows, slab_cols = pair_act.shape
    cells = slab_rows * slab_cols
    tiles = cells // LANES
    flat = pair_act.reshape(chan, 2, tiles, slab_cols).transpose(0, 2, 1, 3).reshape(chan, cells)
    vmem = pl.BlockSpec(memory_space=pltpu.VMEM)
    sems = pltpu.SemaphoreType.DMA
    out = pl.pallas_call(
        functools.partial(fused_kernel, rows),
        out_shape=jax.ShapeDtypeStruct((chan, cells), jnp.bfloat16),
        in_specs=[pl.BlockSpec(memory_space=pl.ANY)] + [vmem] * 9,
        out_specs=vmem,
        scratch_shapes=[
            pltpu.VMEM((2 * chan, cells), jnp.bfloat16),
            pltpu.VMEM((6 * HALF, LANES), jnp.bfloat16),
            pltpu.VMEM((768, LANES), jnp.float32),
            pltpu.VMEM((LANES, LANES), jnp.float32),
            pltpu.VMEM((chan, cells), jnp.float32),
            pltpu.VMEM((dests, tiles * 16, LANES), jnp.bfloat16),
            pltpu.VMEM((dests, tiles * 16, LANES), jnp.bfloat16),
            pltpu.VMEM((2, tiles * 16, LANES), jnp.float32),
            pltpu.VMEM((16, LANES, LANES), jnp.bfloat16),
            pltpu.VMEM((dests, tiles * 8, LANES), jnp.float32),
            pltpu.VMEM((dests, tiles * 8, LANES), jnp.bfloat16),
            pltpu.VMEM((2, dests, tiles * 8, LANES), jnp.bfloat16),
            sems,
            sems((CHUNKS,)),
            sems((CHUNKS,)),
            sems((dests, CHUNKS)),
            sems((dests, CHUNKS)),
            sems((dests,)),
            sems((dests,)),
            sems((dests,)),
            sems((dests,)),
        ],
        compiler_params=pltpu.CompilerParams(
            collective_id=0, has_side_effects=True, vmem_limit_bytes=32 * 1024 * 1024
        ),
        name="triangle_update",
    )(
        flat,
        token_mask.reshape(1, -1),
        norm_gain.reshape(1, -1),
        norm_shift.reshape(1, -1),
        proj_weight,
        gate_weight,
        outgate_weight,
        post_gain.reshape(1, -1),
        post_shift.reshape(1, -1),
        out_weight,
    )
    return out.reshape(chan, tiles, 2, slab_cols).transpose(0, 2, 1, 3).reshape(pair_act.shape)


def solution(mesh):
    placed = (P("ch", ("grp", "row"), "sub"), P("grp"), P(), P(), P(), P(), P(), P(), P(), P())

    def update(*arguments):
        channels, all_rows, tokens = arguments[0].shape
        hidden = arguments[-1].shape[0]
        sizes = dict(mesh.shape)
        fits = (
            (channels, hidden, tokens) == (128, 128, 128)
            and (sizes["row"], sizes["ch"], sizes["sub"]) == (4, 2, 2)
            and all_rows == tokens * sizes["grp"]
        )
        return jax.shard_map(
            fused_body if fits else body,
            mesh=mesh,
            in_specs=placed,
            out_specs=P("ch", ("grp", "row"), "sub"),
            check_vma=False,
        )(*arguments)

    return update
```

```python
import functools

import jax
import jax.numpy as jnp
from jax import lax
from jax.experimental import pallas as pl
from jax.experimental.pallas import tpu as pltpu
from jax.sharding import PartitionSpec as P


def layer_norm(values, gain, shift):
    widened = values.astype(jnp.float32)
    average = jnp.mean(widened, axis=0, keepdims=True)
    centered = widened - average
    variance = jnp.mean(centered * centered, axis=0, keepdims=True)
    scaled = centered * lax.rsqrt(variance + 1e-05)
    spread = (gain.shape[0],) + (1,) * (values.ndim - 1)
    return (scaled * gain.reshape(spread) + shift.reshape(spread)).astype(jnp.bfloat16)


def gated_inputs(normed, weights, pair_mask, hidden):
    projected = jnp.einsum("ce,c...->e...", weights, normed, preferred_element_type=jnp.float32)
    left_panel = (
        projected[:hidden] * jax.nn.sigmoid(projected[2 * hidden : 3 * hidden]) * pair_mask
    ).astype(jnp.bfloat16)
    right_panel = (
        projected[hidden : 2 * hidden]
        * jax.nn.sigmoid(projected[3 * hidden : 4 * hidden])
        * pair_mask
    ).astype(jnp.bfloat16)
    outgate = jax.nn.sigmoid(projected[4 * hidden :])
    return (left_panel, right_panel, outgate)


def contract(left_panel, right_panel):
    partial_sums = jnp.einsum(
        "hik,hjk->hij",
        left_panel,
        lax.all_gather(right_panel, "row", axis=1, tiled=True),
        preferred_element_type=jnp.float32,
    )
    return lax.psum_scatter(partial_sums, "sub", scatter_dimension=2, tiled=True).astype(
        jnp.bfloat16
    )


def body(
    pair_act,
    token_mask,
    norm_gain,
    norm_shift,
    proj_weight,
    gate_weight,
    outgate_weight,
    post_gain,
    post_shift,
    out_weight,
):
    slab_rows = pair_act.shape[1]
    slab_cols = pair_act.shape[2]
    hidden = out_weight.shape[0]
    channels = out_weight.shape[1]
    chan_count = lax.axis_size("ch")
    chan_index = lax.axis_index("ch")
    masked = token_mask.astype(jnp.float32)
    row_mask = lax.dynamic_slice_in_dim(masked, lax.axis_index("row") * slab_rows, slab_rows, 0)
    col_start = lax.axis_index("sub") * slab_cols
    gathered = lax.all_gather(pair_act, "ch", axis=0, tiled=True)
    normed = layer_norm(gathered, norm_gain, norm_shift)
    col_mask = lax.dynamic_slice_in_dim(masked, col_start, slab_cols, 0)
    pair_mask = row_mask[:, None] * col_mask[None, :]
    hid_part = hidden // chan_count
    out_part = channels // chan_count
    hid_start = chan_index * hid_part
    out_start = chan_index * out_part
    weights = jnp.concatenate(
        [
            lax.dynamic_slice_in_dim(proj_weight, hid_start, hid_part, 1),
            lax.dynamic_slice_in_dim(proj_weight, hidden + hid_start, hid_part, 1),
            lax.dynamic_slice_in_dim(gate_weight, hid_start, hid_part, 1),
            lax.dynamic_slice_in_dim(gate_weight, hidden + hid_start, hid_part, 1),
            lax.dynamic_slice_in_dim(outgate_weight, out_start, out_part, 1),
        ],
        axis=1,
    )
    left_panel, right_panel, outgate = gated_inputs(normed, weights, pair_mask, hid_part)
    triangle = contract(left_panel, right_panel)
    all_hidden = lax.all_gather(triangle, "ch", axis=0, tiled=True)
    post = layer_norm(all_hidden, post_gain, post_shift)
    out_slice = lax.dynamic_slice_in_dim(out_weight, out_start, out_part, 1)
    projected_out = jnp.einsum("hc,hij->cij", out_slice, post, preferred_element_type=jnp.float32)
    return (projected_out * outgate).astype(jnp.bfloat16)


MESH = pl.DeviceIdType.MESH
LANES = 128
HALF = 64
CHUNKS = 4


def column(row):
    return jnp.transpose(jnp.broadcast_to(row.astype(jnp.float32), (LANES, LANES)))


def spread_gain(panel, lanes):
    return jnp.concatenate([panel] * (lanes // LANES), axis=1)


def swish_gate(values):
    return 0.5 * jnp.tanh(0.5 * values) + 0.5


def normalise(values, gain, shift):
    average = jnp.mean(values, axis=0, keepdims=True)
    centered = values - average
    variance = jnp.mean(centered * centered, axis=0, keepdims=True)
    scaled = centered * lax.rsqrt(variance + 1e-05)
    return (scaled * gain + shift).astype(jnp.bfloat16)


def fused_kernel(
    rows,
    x_ref,
    mask_ref,
    norm_gain,
    norm_shift,
    proj_ref,
    gate_ref,
    outgate_ref,
    post_gain,
    post_shift,
    out_weight,
    o_ref,
    x_all,
    weights,
    turned,
    wide_weights,
    columns,
    gate_keep,
    send_buf,
    recv_buf,
    wide,
    panels,
    natural,
    tri_wide,
    tri_send,
    tri_all,
    local_sem,
    x_send,
    x_recv,
    a_send,
    a_recv,
    t_send,
    t_recv,
    f_send,
    f_recv,
):
    row = lax.axis_index("row")
    ch = lax.axis_index("ch")
    sub = lax.axis_index("sub")
    dests = 2 * rows
    me = row * 2 + sub
    other_ch = 1 - ch
    tiles = x_ref.shape[1] // LANES
    per = tiles // CHUNKS
    width = per * LANES

    near = row + 1 - 2 * lax.rem(row, 2)
    peers = []
    for there in (lax.rem(row + 2, rows), rows - 1 - row, near, row):
        for core in (sub, 1 - sub):
            peers.append((there * 2 + core, {"row": there, "sub": core}))
    peers = peers[:6] + peers[7:]

    barrier = pltpu.get_barrier_semaphore()
    pl.semaphore_signal(barrier, inc=1, device_id={"ch": other_ch}, device_id_type=MESH)
    for _, where in peers:
        pl.semaphore_signal(barrier, inc=1, device_id=where, device_id_type=MESH)

    own_rows = pl.ds(pl.multiple_of(ch * HALF, HALF), HALF)
    local = pltpu.make_async_copy(x_ref, x_all.at[own_rows], local_sem)
    local.start()
    pl.semaphore_wait(barrier, dests)
    x_copies = []
    for k in range(CHUNKS):
        cells = pl.ds(k * width, width)
        copy = pltpu.make_async_remote_copy(
            src_ref=x_ref.at[:, cells],
            dst_ref=x_all.at[own_rows, cells],
            send_sem=x_send.at[k],
            recv_sem=x_recv.at[k],
            device_id={"ch": other_ch},
            device_id_type=MESH,
        )
        copy.start()
        x_copies.append(copy)

    for at, ref in ((0, proj_ref), (256, gate_ref), (512, outgate_ref), (640, out_weight)):
        turned[at : at + ref.shape[1], :] = jnp.transpose(ref[...].astype(jnp.float32))
    sublane = lax.broadcasted_iota(jnp.int32, (8, LANES), 0)
    upper = sublane < 4
    for slot, base in ((0, 0), (1, 256)):
        for m in range(dests):
            at = pl.multiple_of(base + ch * HALF, HALF) + 8 * m
            left = turned[pl.ds(at, 8), :]
            right = turned[pl.ds(at + 128, 8), :]
            first = jnp.where(upper, left, pltpu.roll(right, 4, 0))
            last = jnp.where(upper, pltpu.roll(left, 4, 0), right)
            wide_weights[128 * slot + 8 * m : 128 * slot + 8 * m + 8, :] = first
            wide_weights[128 * slot + HALF + 8 * m : 128 * slot + HALF + 8 * m + 8, :] = last
    weights[:256, :] = wide_weights[...].astype(jnp.bfloat16)
    for slot, base in ((4, 512), (5, 640)):
        rows_here = pl.ds(pl.multiple_of(base + ch * HALF, HALF), HALF)
        weights[slot * HALF : (slot + 1) * HALF, :] = turned[rows_here, :].astype(jnp.bfloat16)
    gain = column(norm_gain[...])
    shift = column(norm_shift[...])
    lane = lax.broadcasted_iota(jnp.int32, (16, LANES), 1)
    low = lane < HALF
    mask_row = mask_ref[...].astype(jnp.float32)
    columns[...] = column(mask_row)
    mask_wide = jnp.broadcast_to(mask_row, (16, LANES))
    mask_turn = pltpu.roll(mask_wide, HALF, 1)
    inner = jnp.where(low, mask_wide, mask_turn)
    outer = jnp.where(low, mask_turn, mask_wide)
    second = sub.astype(jnp.float32)
    col_mask = inner * (1.0 - second) + outer * second
    row_at = pl.multiple_of(row * 32, 32)
    even = columns[pl.ds(row_at, 16, stride=2), :]
    odd = columns[pl.ds(row_at + 1, 16, stride=2), :]
    row_mask = jnp.where(low, even, odd)
    pair_mask = row_mask * col_mask

    local.wait()
    gain_wide = spread_gain(gain, width)
    shift_wide = spread_gain(shift, width)
    a_copies = [[], []]

    def send_panels(part, piece, first, count):
        span = pl.ds(first * 8, count * 8)
        for p, (d, where) in enumerate(peers):
            copy = pltpu.make_async_remote_copy(
                src_ref=send_buf.at[part, d, span],
                dst_ref=recv_buf.at[part, me, span],
                send_sem=a_send.at[part, p, piece],
                recv_sem=a_recv.at[part, p, piece],
                device_id=where,
                device_id_type=MESH,
            )
            copy.start()
            a_copies[part].append(copy)

    for k in range(CHUNKS):
        cells = pl.ds(k * width, width)
        x_copies[k].wait_recv()
        normed = normalise(x_all[:, cells].astype(jnp.float32), gain_wide, shift_wide)
        projected = jnp.dot(weights[: 5 * HALF, :], normed, preferred_element_type=jnp.float32)
        gate_keep[:, cells] = swish_gate(projected[4 * HALF :])
        both = projected[: 2 * HALF] * swish_gate(projected[2 * HALF : 4 * HALF])
        for t in range(0, per, 2):
            tile = k * per + t
            one = both[:, t * LANES : (t + 1) * LANES] * pair_mask[tile : tile + 1, :]
            two = both[:, (t + 1) * LANES : (t + 2) * LANES] * pair_mask[tile + 1 : tile + 2, :]
            for part in range(2):
                for d in range(dests):
                    at = HALF * part + 8 * d
                    pair = jnp.concatenate([one[at : at + 8], two[at : at + 8]], axis=0)
                    send_buf[part, d, tile * 8 : tile * 8 + 16, :] = pair.astype(jnp.bfloat16)
        send_panels(0, k, k * per, per)
        if k == 0:
            send_panels(1, 0, 0, per)
    send_panels(1, 1, per, tiles - per)
    for part in range(2):
        recv_buf[part, me] = send_buf[part, me]
    post_gain_wide = spread_gain(column(post_gain[...]), width)
    post_shift_wide = spread_gain(column(post_shift[...]), width)

    def products(part):
        for copy in a_copies[part]:
            copy.wait_recv()
        for r in range(rows):
            for s in range(2):
                wide[s] = recv_buf[part, 2 * r + s].astype(jnp.float32)
            for e in range(8):
                first = wide[0, pl.ds(e, 16, stride=8), :]
                last = wide[1, pl.ds(e, 16, stride=8), :]
                top = jnp.where(low, first, pltpu.roll(last, HALF, 1))
                bottom = jnp.where(low, pltpu.roll(first, HALF, 1), last)
                if e < 4:
                    panels[part, e, 32 * r : 32 * r + 16, :] = top.astype(jnp.bfloat16)
                    panels[part, e, 32 * r + 16 : 32 * r + 32, :] = bottom.astype(jnp.bfloat16)
                else:
                    natural[e - 4, pl.ds(32 * r, 16, stride=2), :] = top
                    natural[e - 4, pl.ds(32 * r + 1, 16, stride=2), :] = bottom
        for h in range(4):
            tri = lax.dot_general(
                panels[part, h],
                natural[h].astype(jnp.bfloat16),
                (((1,), (1,)), ((), ())),
                preferred_element_type=jnp.float32,
            )
            rolled = pltpu.roll(tri, HALF, 1)
            for r in range(rows):
                a, b = slice(32 * r, 32 * r + 16), slice(32 * r + 16, 32 * r + 32)
                tri_wide[2 * r, pl.ds(h, 16, stride=4), :] = jnp.where(low, tri[a], rolled[b])
                tri_wide[2 * r + 1, pl.ds(h, 16, stride=4), :] = jnp.where(low, rolled[a], tri[b])
        tri_send[part] = tri_wide[...].astype(jnp.bfloat16)

    t_copies = [[], []]
    f_copies = []

    def send_products(part):
        for p, (d, where) in enumerate(peers):
            copy = pltpu.make_async_remote_copy(
                src_ref=tri_send.at[part, d],
                dst_ref=tri_all.at[ch, part, me],
                send_sem=t_send.at[part, p],
                recv_sem=t_recv.at[part, p],
                device_id=where,
                device_id_type=MESH,
            )
            copy.start()
            t_copies[part].append(copy)
        tri_all[ch, part, me] = tri_send[part, me]

    def forward(part):
        sources = [me] + [d for d, _ in peers]
        for p, source in enumerate(sources):
            if p > 0:
                t_copies[part][p - 1].wait_recv()
            copy = pltpu.make_async_remote_copy(
                src_ref=tri_all.at[ch, part, source],
                dst_ref=tri_all.at[ch, part, source],
                send_sem=f_send.at[part, p],
                recv_sem=f_recv.at[part, p],
                device_id={"ch": other_ch},
                device_id_type=MESH,
            )
            copy.start()
            f_copies.append(copy)

    products(0)
    send_products(0)
    products(1)
    send_products(1)
    forward(0)
    forward(1)
    for copy in f_copies:
        copy.wait_recv()

    for k in range(CHUNKS):
        cells = pl.ds(k * width, width)
        parts = []
        for t in range(k * per, (k + 1) * per, 2):
            evens, odds = [], []
            for c in range(2):
                for q in range(dests):
                    one = tri_all[c, 0, q, t * 4 : t * 4 + 8, :].astype(jnp.float32)
                    two = tri_all[c, 1, q, t * 4 : t * 4 + 8, :].astype(jnp.float32)
                    evens.append(jnp.where(upper, one, pltpu.roll(two, 4, 0)))
                    odds.append(jnp.where(upper, pltpu.roll(one, 4, 0), two))
            parts.append(jnp.concatenate(evens, axis=0))
            parts.append(jnp.concatenate(odds, axis=0))
        post = normalise(jnp.concatenate(parts, axis=1), post_gain_wide, post_shift_wide)
        update = jnp.dot(weights[5 * HALF :, :], post, preferred_element_type=jnp.float32)
        o_ref[:, cells] = (update * gate_keep[:, cells]).astype(jnp.bfloat16)
    for copy in x_copies + a_copies[0] + a_copies[1] + t_copies[0] + t_copies[1] + f_copies:
        copy.wait_send()


def fused_body(
    pair_act,
    token_mask,
    norm_gain,
    norm_shift,
    proj_weight,
    gate_weight,
    outgate_weight,
    post_gain,
    post_shift,
    out_weight,
):
    rows = lax.axis_size("row")
    dests = 2 * rows
    chan, slab_rows, slab_cols = pair_act.shape
    cells = slab_rows * slab_cols
    tiles = cells // LANES
    flat = pair_act.reshape(chan, cells)
    vmem = pl.BlockSpec(memory_space=pltpu.VMEM)
    sems = pltpu.SemaphoreType.DMA
    out = pl.pallas_call(
        functools.partial(fused_kernel, rows),
        out_shape=jax.ShapeDtypeStruct((chan, cells), jnp.bfloat16),
        in_specs=[pl.BlockSpec(memory_space=pl.ANY)] + [vmem] * 9,
        out_specs=vmem,
        scratch_shapes=[
            pltpu.VMEM((2 * chan, cells), jnp.bfloat16),
            pltpu.VMEM((6 * HALF, LANES), jnp.bfloat16),
            pltpu.VMEM((768, LANES), jnp.float32),
            pltpu.VMEM((4 * HALF, LANES), jnp.float32),
            pltpu.VMEM((LANES, LANES), jnp.float32),
            pltpu.VMEM((chan, cells), jnp.float32),
            pltpu.VMEM((2, dests, tiles * 8, LANES), jnp.bfloat16),
            pltpu.VMEM((2, dests, tiles * 8, LANES), jnp.bfloat16),
            pltpu.VMEM((2, tiles * 8, LANES), jnp.float32),
            pltpu.VMEM((2, 4, LANES, LANES), jnp.bfloat16),
            pltpu.VMEM((4, LANES, LANES), jnp.float32),
            pltpu.VMEM((dests, tiles * 4, LANES), jnp.float32),
            pltpu.VMEM((2, dests, tiles * 4, LANES), jnp.bfloat16),
            pltpu.VMEM((2, 2, dests, tiles * 4, LANES), jnp.bfloat16),
            sems,
            sems((CHUNKS,)),
            sems((CHUNKS,)),
            sems((2, dests, CHUNKS)),
            sems((2, dests, CHUNKS)),
            sems((2, dests)),
            sems((2, dests)),
            sems((2, dests)),
            sems((2, dests)),
        ],
        compiler_params=pltpu.CompilerParams(
            collective_id=0, has_side_effects=True, vmem_limit_bytes=32 * 1024 * 1024
        ),
        name="triangle_update",
    )(
        flat,
        token_mask.reshape(1, -1),
        norm_gain.reshape(1, -1),
        norm_shift.reshape(1, -1),
        proj_weight,
        gate_weight,
        outgate_weight,
        post_gain.reshape(1, -1),
        post_shift.reshape(1, -1),
        out_weight,
    )
    return out.reshape(pair_act.shape)


def solution(mesh):
    placed = (P("ch", ("grp", "row"), "sub"), P("grp"), P(), P(), P(), P(), P(), P(), P(), P())

    def update(*arguments):
        channels, all_rows, tokens = arguments[0].shape
        hidden = arguments[-1].shape[0]
        sizes = dict(mesh.shape)
        fits = (
            (channels, hidden, tokens) == (128, 128, 128)
            and (sizes["row"], sizes["ch"], sizes["sub"]) == (4, 2, 2)
            and all_rows == tokens * sizes["grp"]
        )
        return jax.shard_map(
            fused_body if fits else body,
            mesh=mesh,
            in_specs=placed,
            out_specs=P("ch", ("grp", "row"), "sub"),
            check_vma=False,
        )(*arguments)

    return update
```

```python
import functools

import jax
import jax.numpy as jnp
from jax import lax
from jax.experimental import pallas as pl
from jax.experimental.pallas import tpu as pltpu
from jax.sharding import PartitionSpec as P


def layer_norm(values, gain, shift):
    widened = values.astype(jnp.float32)
    average = jnp.mean(widened, axis=0, keepdims=True)
    centered = widened - average
    variance = jnp.mean(centered * centered, axis=0, keepdims=True)
    scaled = centered * lax.rsqrt(variance + 1e-05)
    spread = (gain.shape[0],) + (1,) * (values.ndim - 1)
    return (scaled * gain.reshape(spread) + shift.reshape(spread)).astype(jnp.bfloat16)


def gated_inputs(normed, weights, pair_mask, hidden):
    projected = jnp.einsum("ce,c...->e...", weights, normed, preferred_element_type=jnp.float32)
    left_panel = (
        projected[:hidden] * jax.nn.sigmoid(projected[2 * hidden : 3 * hidden]) * pair_mask
    ).astype(jnp.bfloat16)
    right_panel = (
        projected[hidden : 2 * hidden]
        * jax.nn.sigmoid(projected[3 * hidden : 4 * hidden])
        * pair_mask
    ).astype(jnp.bfloat16)
    outgate = jax.nn.sigmoid(projected[4 * hidden :])
    return (left_panel, right_panel, outgate)


def contract(left_panel, right_panel):
    partial_sums = jnp.einsum(
        "hik,hjk->hij",
        left_panel,
        lax.all_gather(right_panel, "row", axis=1, tiled=True),
        preferred_element_type=jnp.float32,
    )
    return lax.psum_scatter(partial_sums, "sub", scatter_dimension=2, tiled=True).astype(
        jnp.bfloat16
    )


def body(
    pair_act,
    token_mask,
    norm_gain,
    norm_shift,
    proj_weight,
    gate_weight,
    outgate_weight,
    post_gain,
    post_shift,
    out_weight,
):
    slab_rows = pair_act.shape[1]
    slab_cols = pair_act.shape[2]
    hidden = out_weight.shape[0]
    channels = out_weight.shape[1]
    chan_count = lax.axis_size("ch")
    chan_index = lax.axis_index("ch")
    masked = token_mask.astype(jnp.float32)
    row_mask = lax.dynamic_slice_in_dim(masked, lax.axis_index("row") * slab_rows, slab_rows, 0)
    col_start = lax.axis_index("sub") * slab_cols
    gathered = lax.all_gather(pair_act, "ch", axis=0, tiled=True)
    normed = layer_norm(gathered, norm_gain, norm_shift)
    col_mask = lax.dynamic_slice_in_dim(masked, col_start, slab_cols, 0)
    pair_mask = row_mask[:, None] * col_mask[None, :]
    hid_part = hidden // chan_count
    out_part = channels // chan_count
    hid_start = chan_index * hid_part
    out_start = chan_index * out_part
    weights = jnp.concatenate(
        [
            lax.dynamic_slice_in_dim(proj_weight, hid_start, hid_part, 1),
            lax.dynamic_slice_in_dim(proj_weight, hidden + hid_start, hid_part, 1),
            lax.dynamic_slice_in_dim(gate_weight, hid_start, hid_part, 1),
            lax.dynamic_slice_in_dim(gate_weight, hidden + hid_start, hid_part, 1),
            lax.dynamic_slice_in_dim(outgate_weight, out_start, out_part, 1),
        ],
        axis=1,
    )
    left_panel, right_panel, outgate = gated_inputs(normed, weights, pair_mask, hid_part)
    triangle = contract(left_panel, right_panel)
    all_hidden = lax.all_gather(triangle, "ch", axis=0, tiled=True)
    post = layer_norm(all_hidden, post_gain, post_shift)
    out_slice = lax.dynamic_slice_in_dim(out_weight, out_start, out_part, 1)
    projected_out = jnp.einsum("hc,hij->cij", out_slice, post, preferred_element_type=jnp.float32)
    return (projected_out * outgate).astype(jnp.bfloat16)


MESH = pl.DeviceIdType.MESH
LANES = 128
HALF = 64
CHUNKS = 4


def column(row):
    return jnp.transpose(jnp.broadcast_to(row.astype(jnp.float32), (LANES, LANES)))


def spread_gain(panel, lanes):
    return jnp.concatenate([panel] * (lanes // LANES), axis=1)


def swish_gate(values):
    return 0.5 * jnp.tanh(0.5 * values) + 0.5


def normalise(values, gain, shift):
    average = jnp.mean(values, axis=0, keepdims=True)
    centered = values - average
    variance = jnp.mean(centered * centered, axis=0, keepdims=True)
    scaled = centered * lax.rsqrt(variance + 1e-05)
    return (scaled * gain + shift).astype(jnp.bfloat16)


def fused_kernel(
    rows,
    x_ref,
    mask_ref,
    norm_gain,
    norm_shift,
    proj_ref,
    gate_ref,
    outgate_ref,
    post_gain,
    post_shift,
    out_weight,
    o_ref,
    x_all,
    weights,
    turned,
    columns,
    gate_keep,
    send_buf,
    recv_buf,
    wide,
    panels,
    natural,
    tri_wide,
    tri_send,
    tri_all,
    local_sem,
    x_send,
    x_recv,
    a_send,
    a_recv,
    t_send,
    t_recv,
    f_send,
    f_recv,
):
    row = lax.axis_index("row")
    ch = lax.axis_index("ch")
    sub = lax.axis_index("sub")
    dests = 2 * rows
    me = row * 2 + sub
    other_ch = 1 - ch
    tiles = x_ref.shape[1] // LANES
    per = tiles // CHUNKS
    width = per * LANES

    near = row + 1 - 2 * lax.rem(row, 2)
    peers = []
    for there in (row, near, lax.rem(row + 2, rows), rows - 1 - row):
        for core in (sub, 1 - sub):
            peers.append((there * 2 + core, {"row": there, "sub": core}))
    peers = peers[1:]

    barrier = pltpu.get_barrier_semaphore()
    pl.semaphore_signal(barrier, inc=1, device_id={"ch": other_ch}, device_id_type=MESH)
    for _, where in peers:
        pl.semaphore_signal(barrier, inc=1, device_id=where, device_id_type=MESH)

    own_rows = pl.ds(pl.multiple_of(ch * HALF, HALF), HALF)
    local = pltpu.make_async_copy(x_ref, x_all.at[own_rows], local_sem)
    local.start()
    pl.semaphore_wait(barrier, dests)
    x_copies = []
    for k in range(CHUNKS):
        cells = pl.ds(k * width, width)
        copy = pltpu.make_async_remote_copy(
            src_ref=x_ref.at[:, cells],
            dst_ref=x_all.at[own_rows, cells],
            send_sem=x_send.at[k],
            recv_sem=x_recv.at[k],
            device_id={"ch": other_ch},
            device_id_type=MESH,
        )
        copy.start()
        x_copies.append(copy)

    for at, ref in ((0, proj_ref), (256, gate_ref), (512, outgate_ref), (640, out_weight)):
        turned[at : at + ref.shape[1], :] = jnp.transpose(ref[...].astype(jnp.float32))
    for slot, base in enumerate((128, 0, 384, 256, 512, 640)):
        rows_here = pl.ds(pl.multiple_of(base + ch * HALF, HALF), HALF)
        weights[slot * HALF : (slot + 1) * HALF, :] = turned[rows_here, :].astype(jnp.bfloat16)
    gain = column(norm_gain[...])
    shift = column(norm_shift[...])
    lane = lax.broadcasted_iota(jnp.int32, (16, LANES), 1)
    low = lane < HALF
    mask_row = mask_ref[...].astype(jnp.float32)
    columns[...] = column(mask_row)
    mask_wide = jnp.broadcast_to(mask_row, (16, LANES))
    mask_turn = pltpu.roll(mask_wide, HALF, 1)
    inner = jnp.where(low, mask_wide, mask_turn)
    outer = jnp.where(low, mask_turn, mask_wide)
    second = sub.astype(jnp.float32)
    col_mask = inner * (1.0 - second) + outer * second
    row_at = pl.multiple_of(row * 32, 32)
    even = columns[pl.ds(row_at, 16, stride=2), :]
    odd = columns[pl.ds(row_at + 1, 16, stride=2), :]
    row_mask = jnp.where(low, even, odd)
    pair_mask = row_mask * col_mask

    local.wait()
    gain_wide = spread_gain(gain, width)
    shift_wide = spread_gain(shift, width)
    a_copies = [[], []]

    def send_panels(part, piece, first, count):
        span = pl.ds(first * 8, count * 8)
        for p, (d, where) in enumerate(peers):
            copy = pltpu.make_async_remote_copy(
                src_ref=send_buf.at[part, d, span],
                dst_ref=recv_buf.at[part, me, span],
                send_sem=a_send.at[part, p, piece],
                recv_sem=a_recv.at[part, p, piece],
                device_id=where,
                device_id_type=MESH,
            )
            copy.start()
            a_copies[part].append(copy)

    for k in range(CHUNKS):
        cells = pl.ds(k * width, width)
        x_copies[k].wait_recv()
        normed = normalise(x_all[:, cells].astype(jnp.float32), gain_wide, shift_wide)
        projected = jnp.dot(weights[: 5 * HALF, :], normed, preferred_element_type=jnp.float32)
        gate_keep[:, cells] = swish_gate(projected[4 * HALF :])
        both = projected[: 2 * HALF] * swish_gate(projected[2 * HALF : 4 * HALF])
        for t in range(0, per, 2):
            tile = k * per + t
            one = both[:, t * LANES : (t + 1) * LANES] * pair_mask[tile : tile + 1, :]
            two = both[:, (t + 1) * LANES : (t + 2) * LANES] * pair_mask[tile + 1 : tile + 2, :]
            for part in range(2):
                for d in range(dests):
                    at = HALF * part + 8 * d
                    pair = jnp.concatenate([one[at : at + 8], two[at : at + 8]], axis=0)
                    send_buf[part, d, tile * 8 : tile * 8 + 16, :] = pair.astype(jnp.bfloat16)
        send_panels(0, k, k * per, per)
        if k == 0:
            send_panels(1, 0, 0, per)
    for k in range(1, CHUNKS):
        send_panels(1, k, k * per, per)
    for part in range(2):
        recv_buf[part, me] = send_buf[part, me]
    post_gain_wide = spread_gain(column(post_gain[...]), width)
    post_shift_wide = spread_gain(column(post_shift[...]), width)

    for copy in a_copies[0]:
        copy.wait_recv()
    for r in range(rows):
        for s in range(2):
            wide[s, : tiles * 8, :] = recv_buf[0, 2 * r + s].astype(jnp.float32)
        for e in range(8):
            first = wide[0, pl.ds(e, 16, stride=8), :]
            last = wide[1, pl.ds(e, 16, stride=8), :]
            even = jnp.where(low, first, pltpu.roll(last, HALF, 1))
            odd = jnp.where(low, pltpu.roll(first, HALF, 1), last)
            natural[e, pl.ds(32 * r, 16, stride=2), :] = even
            natural[e, pl.ds(32 * r + 1, 16, stride=2), :] = odd
    panels[...] = natural[...].astype(jnp.bfloat16)

    block_rows = per * 8
    count = rows * per
    wide_low = lax.broadcasted_iota(jnp.int32, (count, LANES), 1) < HALF
    t_copies, f_copies = [], []

    def products(k):
        for p in range(dests - 1):
            a_copies[1][k * (dests - 1) + p].wait_recv()
        for r in range(rows):
            for s in range(2):
                part = recv_buf[1, 2 * r + s, k * block_rows : (k + 1) * block_rows, :]
                wide[s, r * block_rows : (r + 1) * block_rows, :] = part.astype(jnp.float32)
        for e in range(8):
            first = wide[0, pl.ds(e, count, stride=8), :]
            last = wide[1, pl.ds(e, count, stride=8), :]
            even = jnp.where(wide_low, first, pltpu.roll(last, HALF, 1))
            odd = jnp.where(wide_low, pltpu.roll(first, HALF, 1), last)
            left = jnp.concatenate([even, odd], axis=0).astype(jnp.bfloat16)
            tri = lax.dot_general(
                left, panels[e], (((1,), (1,)), ((), ())), preferred_element_type=jnp.float32
            )
            rolled = pltpu.roll(tri, HALF, 1)
            tri_wide[0, pl.ds(e, count, stride=8), :] = jnp.where(
                wide_low, tri[:count], rolled[count:]
            )
            tri_wide[1, pl.ds(e, count, stride=8), :] = jnp.where(
                wide_low, rolled[:count], tri[count:]
            )
        for r in range(rows):
            for s in range(2):
                part = tri_wide[s, r * block_rows : (r + 1) * block_rows, :]
                tri_send[k, 2 * r + s] = part.astype(jnp.bfloat16)
        for p, (d, where) in enumerate(peers):
            copy = pltpu.make_async_remote_copy(
                src_ref=tri_send.at[k, d],
                dst_ref=tri_all.at[ch, k, me],
                send_sem=t_send.at[k, p],
                recv_sem=t_recv.at[k, p],
                device_id=where,
                device_id_type=MESH,
            )
            copy.start()
            t_copies.append(copy)
        tri_all[ch, k, me] = tri_send[k, me]
        forward(k, dests - 1, me)

    def forward(k, slot, source):
        copy = pltpu.make_async_remote_copy(
            src_ref=tri_all.at[ch, k, source],
            dst_ref=tri_all.at[ch, k, source],
            send_sem=f_send.at[k, slot],
            recv_sem=f_recv.at[k, slot],
            device_id={"ch": other_ch},
            device_id_type=MESH,
        )
        copy.start()
        f_copies[k].append(copy)

    def forward_all(k):
        for p in range(dests - 1):
            t_copies[k * (dests - 1) + p].wait_recv()
            forward(k, p, peers[p][0])

    def finish(k):
        for copy in f_copies[k]:
            copy.wait_recv()
        cells = pl.ds(k * width, width)
        parts = []
        for t in range(per):
            stack = [
                tri_all[c, k, q, t * 8 : t * 8 + 8, :].astype(jnp.float32)
                for c in range(2)
                for q in range(dests)
            ]
            parts.append(jnp.concatenate(stack, axis=0))
        post = normalise(jnp.concatenate(parts, axis=1), post_gain_wide, post_shift_wide)
        update = jnp.dot(weights[5 * HALF :, :], post, preferred_element_type=jnp.float32)
        o_ref[:, cells] = (update * gate_keep[:, cells]).astype(jnp.bfloat16)

    for k in range(CHUNKS):
        f_copies.append([])
        products(k)
        if k > 1:
            forward_all(k - 2)
    for k in range(CHUNKS - 2, CHUNKS):
        forward_all(k)
        finish(k - 2)
    finish(CHUNKS - 2)
    finish(CHUNKS - 1)
    for copy in x_copies + a_copies[0] + a_copies[1] + t_copies + sum(f_copies, []):
        copy.wait_send()


def fused_body(
    pair_act,
    token_mask,
    norm_gain,
    norm_shift,
    proj_weight,
    gate_weight,
    outgate_weight,
    post_gain,
    post_shift,
    out_weight,
):
    rows = lax.axis_size("row")
    dests = 2 * rows
    chan, slab_rows, slab_cols = pair_act.shape
    cells = slab_rows * slab_cols
    tiles = cells // LANES
    block = tiles // CHUNKS * 8
    flat = pair_act.reshape(chan, cells)
    vmem = pl.BlockSpec(memory_space=pltpu.VMEM)
    sems = pltpu.SemaphoreType.DMA
    out = pl.pallas_call(
        functools.partial(fused_kernel, rows),
        out_shape=jax.ShapeDtypeStruct((chan, cells), jnp.bfloat16),
        in_specs=[pl.BlockSpec(memory_space=pl.ANY)] + [vmem] * 9,
        out_specs=vmem,
        scratch_shapes=[
            pltpu.VMEM((2 * chan, cells), jnp.bfloat16),
            pltpu.VMEM((6 * HALF, LANES), jnp.bfloat16),
            pltpu.VMEM((768, LANES), jnp.float32),
            pltpu.VMEM((LANES, LANES), jnp.float32),
            pltpu.VMEM((chan, cells), jnp.float32),
            pltpu.VMEM((2, dests, tiles * 8, LANES), jnp.bfloat16),
            pltpu.VMEM((2, dests, tiles * 8, LANES), jnp.bfloat16),
            pltpu.VMEM((2, max(tiles * 8, rows * block), LANES), jnp.float32),
            pltpu.VMEM((8, LANES, LANES), jnp.bfloat16),
            pltpu.VMEM((8, LANES, LANES), jnp.float32),
            pltpu.VMEM((2, rows * block, LANES), jnp.float32),
            pltpu.VMEM((CHUNKS, dests, block, LANES), jnp.bfloat16),
            pltpu.VMEM((2, CHUNKS, dests, block, LANES), jnp.bfloat16),
            sems,
            sems((CHUNKS,)),
            sems((CHUNKS,)),
            sems((2, dests, CHUNKS)),
            sems((2, dests, CHUNKS)),
            sems((CHUNKS, dests)),
            sems((CHUNKS, dests)),
            sems((CHUNKS, dests)),
            sems((CHUNKS, dests)),
        ],
        compiler_params=pltpu.CompilerParams(
            collective_id=0, has_side_effects=True, vmem_limit_bytes=32 * 1024 * 1024
        ),
        name="triangle_update",
    )(
        flat,
        token_mask.reshape(1, -1),
        norm_gain.reshape(1, -1),
        norm_shift.reshape(1, -1),
        proj_weight,
        gate_weight,
        outgate_weight,
        post_gain.reshape(1, -1),
        post_shift.reshape(1, -1),
        out_weight,
    )
    return out.reshape(pair_act.shape)


def solution(mesh):
    placed = (P("ch", ("grp", "row"), "sub"), P("grp"), P(), P(), P(), P(), P(), P(), P(), P())

    def update(*arguments):
        channels, all_rows, tokens = arguments[0].shape
        hidden = arguments[-1].shape[0]
        sizes = dict(mesh.shape)
        fits = (
            (channels, hidden, tokens) == (128, 128, 128)
            and (sizes["row"], sizes["ch"], sizes["sub"]) == (4, 2, 2)
            and all_rows == tokens * sizes["grp"]
        )
        return jax.shard_map(
            fused_body if fits else body,
            mesh=mesh,
            in_specs=placed,
            out_specs=P("ch", ("grp", "row"), "sub"),
            check_vma=False,
        )(*arguments)

    return update
```
